256 devices in a mesh: queue: 32 (over z_hi, y, core), head: 8 (over z_lo, x).
Axes of the slice: x: 4, y: 4, z: 8 (z_hi: 4, z_lo: 2; z = z_hi * 2 + z_lo), core: 2. Of those that a mesh axis runs over, the one named last changes fastest.
Arguments:
- latents: bfloat16 [9216, 3072], P('queue'), may hold values from -6 to 6
- levels: int32 [32], P('queue'), may hold values from 0 to 15
- counts: int32 [32], replicated, may hold values from 72 to 288, as said below
- window_mask: int32 [32, 2], replicated, may hold values 0 or 1
- modulation: float32 [16, 9216], replicated, may hold values from -1 to 25, as said below
- qkv_weight: bfloat16 [3072, 3, 3072], P(None, None, 'head'), may hold values from -0.109375 to 0.109375
- out_weight: bfloat16 [3072, 3072], P('head'), may hold values from -0.109375 to 0.109375
Outputs:
- queue_next: bfloat16 [9216, 3072], P('queue')
The draws below stay inside these ranges and needn't reach their ends.
Inputs may be any that keep to these rules, and one draw needn't show every extreme that they name: `counts`: at least one span has exactly 288 valid tokens and at least one has 72. `modulation`: gates and shifts lie in -1 to 1.5; scales of some levels may be large.
All inputs are finite; a program needn't handle non-finite values.
Results may differ from the reference program's by a relative error of at most 0.03.
The reference program's roundings to bfloat16 on the way count: a program that leaves them out, or rounds other values in their place, can miss the bound.
Values may be sent and summed in bfloat16 or wider, within the bound.
No kernel may reach another device: no remote copies, remote signals or barrier semaphores. Data moves between devices by JAX's collectives and lax.ppermute only.
A program may use at most 128 MiB of HBM per device.

```python
import math
import jax
import jax.numpy as jnp
from jax import lax

D = 3072
HEADS = 24
HD = 128
TOK_DEV = 288
LEVELS = 16
SPANS = 32
ROWS = 9216
N_HEAD = 8


def draw_counts(key, part):
    key = jax.random.fold_in(key, 2)
    first, second = jax.random.split(key)
    base = jax.random.randint(first, (SPANS,), TOK_DEV // 4, TOK_DEV + 1)
    order = jax.random.permutation(second, SPANS)
    base = base.at[order[0]].set(TOK_DEV)
    base = base.at[order[1]].set(TOK_DEV // 4)
    return base.astype(jnp.int32)


def draw_modulation(key, part):
    key = jax.random.fold_in(key, 5)
    keys = jax.random.split(key, 3)
    shift = jax.random.uniform(keys[0], (LEVELS, D), jnp.float32, -1.0, 1.0)
    scale = jax.random.uniform(keys[1], (LEVELS, D), jnp.float32, -0.5, 1.0)
    gate = jax.random.uniform(keys[2], (LEVELS, D), jnp.float32, 0.5, 1.5)
    return jnp.concatenate([shift, scale, gate], axis=1).astype(jnp.float32)


def with_ends(array, stream_key, smallest, top_value):
    longest = array.shape.index(max(array.shape))
    spots = []
    for shift in (0, 1):
        where = [jax.random.randint(jax.random.fold_in(stream_key, axis), (), 0, length) for axis, length in enumerate(array.shape)]
        where[longest] = (where[longest] + shift) % array.shape[longest]
        spots.append(tuple(where))
    return array.at[spots[0]].set(smallest).at[spots[1]].set(top_value)


def steps_of(rng, extent, pieces, least, top_value):
    def one(position, shards_of):
        steps = jax.random.uniform(jax.random.fold_in(jax.random.fold_in(rng, 6), position), (shards_of,), jnp.float32, least / len(pieces), top_value / len(pieces))
        return jnp.repeat(jnp.exp(steps), extent[position] // shards_of).reshape((-1,) + (1,) * (len(extent) - position - 1))

    loudness = one(*pieces[0])
    for cut in pieces[1:]:
        loudness = loudness * one(*cut)
    return loudness


def centred(own_key, dims, deviation, most, cuts=(), dtype=jnp.bfloat16):
    array = jax.random.normal(own_key, dims, jnp.float32) * deviation
    if len(cuts) > 0:
        array = steps_of(own_key, dims, cuts, -0.22, 0.18) * array
    return jnp.clip(array, min=-most, max=most).astype(dtype)


def setup_inputs(seed: int = 0) -> dict:
    key_of = jax.random.split(jax.random.key(seed), 8)
    return {
        "latents": centred(key_of[0], (ROWS, D), 1.0, 6.0, ((0, 32),)),
        "levels": with_ends(jax.random.randint(key_of[1], (SPANS,), 0, LEVELS), jax.random.fold_in(key_of[1], 1), 0, LEVELS - 1).astype(jnp.int32),
        "counts": draw_counts(jax.random.fold_in(key_of[7], 71), 0),
        "window_mask": with_ends((jax.random.randint(key_of[3], (SPANS, 2), 0, 4) < 3).astype(jnp.int32), jax.random.fold_in(key_of[3], 1), 0, 1),
        "modulation": draw_modulation(jax.random.fold_in(key_of[7], 71), 0),
        "qkv_weight": centred(key_of[5], (D, 3, HEADS * HD), D ** -0.5, 0.109375, ((2, 8),)),
        "out_weight": centred(key_of[6], (HEADS * HD, D), (HEADS * HD) ** -0.5, 0.109375, ((0, 8),)),
    }


def normalize(rows, shift, scale):
    mean = lax.optimization_barrier(jnp.mean(rows, axis=-1, keepdims=True))
    centered = rows - mean
    variance = lax.optimization_barrier(jnp.mean(centered * centered, axis=-1, keepdims=True))
    return centered / jnp.sqrt(variance + 1e-06) * (1.0 + scale) + shift

def attend_span(query, keys, values, limits):
    scores = jnp.einsum('thd,shd->hts', query.astype(jnp.float32), keys.astype(jnp.float32)) / math.sqrt(HD)
    spots = jnp.arange(3 * TOK_DEV)
    limit = jnp.where(spots // TOK_DEV == 0, limits[0], jnp.where(spots // TOK_DEV == 1, limits[1], limits[2]))
    valid = spots % TOK_DEV < limit
    scores = jnp.where(valid[None, None, :], scores, -jnp.inf)
    top = lax.optimization_barrier(jnp.max(scores, axis=-1, keepdims=True))
    expo = jnp.exp(scores - top)
    weights = (expo / lax.optimization_barrier(jnp.sum(expo, axis=-1, keepdims=True))).astype(jnp.bfloat16)
    out = jnp.einsum('hts,shd->thd', weights.astype(jnp.float32), values.astype(jnp.float32))
    return out.astype(jnp.bfloat16)

def reference(latents, levels, counts, window_mask, modulation, qkv_weight, out_weight):
    span_rows = latents.astype(jnp.float32).reshape(SPANS, TOK_DEV, D)
    table = jnp.take(modulation, levels, axis=0)
    shift = table[:, None, :D]
    scale = table[:, None, D:2 * D]
    gate = table[:, None, 2 * D:]
    normed = normalize(span_rows, shift, scale).astype(jnp.bfloat16)
    widthq = HEADS * HD
    qkv = jnp.dot(normed.reshape(ROWS, D), qkv_weight.reshape(D, 3 * widthq), preferred_element_type=jnp.float32)
    qkv = qkv.astype(jnp.bfloat16).reshape(SPANS, TOK_DEV, 3, HEADS, HD)
    query = qkv[:, :, 0]
    keys = qkv[:, :, 1]
    values = qkv[:, :, 2]
    blank = jnp.zeros_like(keys[:1])
    keys_all = jnp.concatenate([jnp.concatenate([blank, keys[:-1]]), keys, jnp.concatenate([keys[1:], blank])], axis=1)
    values_all = jnp.concatenate([jnp.concatenate([blank, values[:-1]]), values, jnp.concatenate([values[1:], blank])], axis=1)
    zero = jnp.zeros((1,), jnp.int32)
    prev_limit = jnp.concatenate([zero, counts[:-1]]) * window_mask[:, 0]
    next_limit = jnp.concatenate([counts[1:], zero]) * window_mask[:, 1]
    limits = jnp.stack([prev_limit, counts, next_limit], axis=1)
    attended = lax.map(lambda item: attend_span(*item), (query, keys_all, values_all, limits))
    attended = attended.reshape(ROWS, widthq)
    group = widthq // N_HEAD
    projected = jnp.zeros((ROWS, D), jnp.float32)
    for index in range(N_HEAD):
        partial_sum = jnp.dot(attended[:, index * group:(index + 1) * group], out_weight[index * group:(index + 1) * group], preferred_element_type=jnp.float32)
        projected = projected + partial_sum.astype(jnp.bfloat16).astype(jnp.float32)
    updated = (span_rows + gate * projected.reshape(SPANS, TOK_DEV, D)).astype(jnp.bfloat16)
    return jnp.roll(updated, -1, axis=0).reshape(ROWS, D)
```

```python
import functools
import math

import jax
import jax.numpy as jnp
from jax import lax
from jax.experimental import pallas as pl
from jax.experimental.pallas import tpu as pltpu
from jax.sharding import PartitionSpec as P

HD = 128
ORDERS = ((4, 1, 3), (1, 3, 4), (3, 4, 1))
CHUNK = 16
F32, BF16 = jnp.float32, jnp.bfloat16


def vmem(n=1):
    return [pl.BlockSpec(memory_space=pltpu.VMEM)] * n


def smem(n=1):
    return [pl.BlockSpec(memory_space=pltpu.SMEM)] * n


def hbm(n=1):
    return [pl.BlockSpec(memory_space=pltpu.HBM)] * n


def params(mib):
    return pltpu.CompilerParams(vmem_limit_bytes=mib * 1024 * 1024)


def cost(flops, size):
    return pl.CostEstimate(flops=flops, bytes_accessed=size, transcendentals=0)


def dot(a, b):
    return jnp.dot(a, b, preferred_element_type=F32)


def dot_t(a, b):
    return lax.dot_general(a, b, (((1,), (1,)), ((), ())), preferred_element_type=F32)


def combos(dims):
    found = [0]
    for d in dims:
        found = [f ^ e for f in found for e in (0, d)]
    return found


def columns(target, size):
    return pl.ds(pl.multiple_of(target * size, size), size)


def keys_kernel(level_ref, x_hbm, mod_hbm, w_hbm, kv_ref, normed_ref, x_ref, mod_ref, w_ref, sems):
    rows, width = x_ref.shape
    level = level_ref[0]
    first = pl.multiple_of(level // 8 * 8, 8)
    copy_x = pltpu.make_async_copy(x_hbm, x_ref, sems.at[0])
    copy_mod = pltpu.make_async_copy(mod_hbm.at[pl.ds(first, 8), pl.ds(0, 2 * width)], mod_ref, sems.at[1])
    copy_k = pltpu.make_async_copy(w_hbm.at[1], w_ref.at[0], sems.at[2])
    copy_v = pltpu.make_async_copy(w_hbm.at[2], w_ref.at[1], sems.at[3])
    copy_x.start()
    copy_mod.start()
    copy_k.start()
    copy_v.start()
    copy_x.wait()
    copy_mod.wait()
    row = pl.ds(level % 8, 1)

    def step(i, carry):
        at = pl.ds(pl.multiple_of(i * CHUNK, CHUNK), CHUNK)
        x = x_ref[at, :].astype(F32)
        mean = jnp.mean(x, axis=-1, keepdims=True)
        centered = x - mean
        variance = jnp.mean(centered * centered, axis=-1, keepdims=True)
        scaled = centered * lax.rsqrt(variance + 1e-06)
        normed = scaled * (1.0 + mod_ref[row, width:]) + mod_ref[row, :width]
        normed_ref[at, :] = normed.astype(BF16)
        return carry

    lax.fori_loop(0, rows // CHUNK, step, 0, unroll=3)
    copy_k.wait()
    kv_ref[0] = dot(normed_ref[...], w_ref[0]).astype(BF16)
    copy_v.wait()
    kv_ref[1] = dot(normed_ref[...], w_ref[1]).astype(BF16)


def masked(scores, limit):
    spots = lax.broadcasted_iota(jnp.int32, scores.shape, 1)
    return jnp.where(spots < limit, scores * (1.0 / math.sqrt(HD)), -jnp.inf)


def self_kernel(
    meta_ref, level_ref, counts_ref, normed_ref, w_hbm, mod_hbm, kv_ref, q_ref, o_ref, m_ref, l_ref, gate_ref, w_ref, mod_ref, sems
):
    rows, width = normed_ref.shape
    level = level_ref[0]
    first = pl.multiple_of(level // 8 * 8, 8)
    copy = pltpu.make_async_copy(w_hbm.at[0], w_ref, sems.at[0])
    copy_mod = pltpu.make_async_copy(
        mod_hbm.at[pl.ds(first, 8), pl.ds(2 * width, width)], mod_ref, sems.at[1]
    )
    copy.start()
    copy_mod.start()
    copy_mod.wait()
    gate_ref[...] = mod_ref[pl.ds(level % 8, 1), :]
    copy.wait()
    q_ref[...] = dot(normed_ref[...], w_ref[...]).astype(BF16)
    limit = counts_ref[meta_ref[0]]
    for head in range(q_ref.shape[1] // HD):
        at = slice(head * HD, (head + 1) * HD)
        scores = masked(dot_t(q_ref[:, at], kv_ref[0, :, at]), limit)
        top = jnp.max(scores, axis=-1, keepdims=True)
        expo = jnp.exp(scores - top)
        m_ref[:, at] = jnp.broadcast_to(top, (rows, HD))
        l_ref[:, at] = jnp.broadcast_to(jnp.sum(expo, axis=-1, keepdims=True), (rows, HD))
        o_ref[:, at] = dot(expo.astype(BF16), kv_ref[1, :, at])


def join_kernel(meta_ref, counts_ref, mask_ref, q_ref, o_ref, m_ref, l_ref, cross_ref, chip_ref, w_ref, *refs):
    outs, att_ref = refs[:-1], refs[-1]
    places = counts_ref.shape[0]
    place, h = meta_ref[0], meta_ref[1]
    before = jnp.where(place > 0, counts_ref[jnp.maximum(place - 1, 0)] * mask_ref[0, place], 0)
    after = jnp.where(
        place < places - 1, counts_ref[jnp.minimum(place + 1, places - 1)] * mask_ref[1, place], 0
    )
    odd = place % 2 == 1
    cross = jnp.where(odd, after, before)
    chip = jnp.where(odd, before, after)
    for head in range(q_ref.shape[1] // HD):
        at = slice(head * HD, (head + 1) * HD)
        query = q_ref[:, at]
        left = masked(dot_t(query, cross_ref[0, :, at]), cross)
        right = masked(dot_t(query, chip_ref[0, :, at]), chip)
        old = m_ref[:, at][:, :1]
        top = jnp.maximum(old, jnp.max(jnp.maximum(left, right), axis=-1, keepdims=True))
        left = jnp.exp(left - top)
        right = jnp.exp(right - top)
        keep = jnp.exp(old - top)
        total = l_ref[:, at][:, :1] * keep + jnp.sum(left + right, axis=-1, keepdims=True)
        acc = o_ref[:, at] * keep
        acc = acc + dot(left.astype(BF16), cross_ref[1, :, at])
        acc = acc + dot(right.astype(BF16), chip_ref[1, :, at])
        att_ref[:, at] = (acc / total).astype(BF16)
    rows, size = q_ref.shape
    part = rows // len(ORDERS)
    for k in range(w_ref.shape[1] // size):
        result = dot(att_ref[...], w_ref[:, columns(h ^ k, size)]).astype(BF16)
        for c, dims in enumerate(ORDERS):
            spot = combos(dims).index(k)
            outs[2 * c + spot // 4][spot % 4] = result[c * part : (c + 1) * part]


def add_kernel(keep_ref, got_ref, *outs):
    total = (keep_ref[...].astype(F32) + got_ref[...].astype(F32)).astype(BF16)
    if len(outs) == 1:
        outs[0][...] = total
    else:
        half = total.shape[0] // 2
        outs[0][...] = total[:half]
        outs[1][...] = total[half:]


def update_kernel(chain, meta_ref, x_ref, gate_ref, keep_ref, got_ref, out_ref):
    part, size = out_ref.shape[1:]
    for c, step in enumerate((0, ORDERS[chain][2])):
        at = columns(meta_ref[1] ^ step, size)
        total = keep_ref[c].astype(F32) + got_ref[1 - c].astype(F32)
        x = x_ref[chain * part : (chain + 1) * part, at].astype(F32)
        out_ref[c] = (x + gate_ref[:, at] * total).astype(BF16)


def concat_kernel(a_ref, b_ref, out_ref):
    half = a_ref.shape[0]
    out_ref[:half] = a_ref[...]
    out_ref[half:] = b_ref[...]


def place_kernel(chain, meta_ref, *refs):
    own_ref, got_ref, out, sems = refs[-4:]
    part, size = own_ref.shape[1:]
    d1, d2, d3 = ORDERS[chain]
    copies = []
    for i, step in enumerate(combos((d1, d2, d3))):
        piece = (own_ref if i < 4 else got_ref).at[i % 4]
        to = out.at[pl.ds(chain * part, part), columns(meta_ref[1] ^ step, size)]
        copies.append(pltpu.make_async_copy(piece, to, sems.at[i]))
        copies[-1].start()
    for copy in copies:
        copy.wait()


def body(latents, levels, counts, window_mask, modulation, qkv_weight, out_weight):
    rows, width = latents.shape
    size = qkv_weight.shape[2]
    part = rows // len(ORDERS)
    weight = jnp.transpose(qkv_weight, (1, 0, 2))
    n_head = lax.axis_size("head")
    n_queue = lax.axis_size("queue")
    meta = jnp.stack([lax.axis_index("queue"), lax.axis_index("head")]).astype(jnp.int32)
    shape = jax.ShapeDtypeStruct

    def swap(array, step):
        return lax.ppermute(array, "head", [(i, i ^ step) for i in range(n_head)])

    kv, normed = pl.pallas_call(
        keys_kernel,
        out_shape=(shape((2, rows, size), BF16), shape((rows, width), BF16)),
        in_specs=smem() + hbm(3),
        out_specs=vmem(2),
        scratch_shapes=[
            pltpu.VMEM((rows, width), BF16),
            pltpu.VMEM((8, 2 * width), F32),
            pltpu.VMEM((2, width, size), BF16),
            pltpu.SemaphoreType.DMA((4,)),
        ],
        compiler_params=params(32),
        cost_estimate=cost(4 * rows * width * size, 4 * width * size),
    )(levels, latents, modulation, weight)

    pairs = [(i, i + 1) for i in range(1, n_queue - 1, 2)]
    cross = lax.ppermute(kv, "queue", pairs + [(j, i) for i, j in pairs])
    pairs = [(i, i + 1) for i in range(0, n_queue, 2)]
    chip = lax.ppermute(kv, "queue", pairs + [(j, i) for i, j in pairs])

    query, acc, top, total, gate = pl.pallas_call(
        self_kernel,
        out_shape=(shape((rows, size), BF16),) + (shape((rows, size), F32),) * 3 + (shape((1, width), F32),),
        in_specs=smem(3) + vmem() + hbm(2) + vmem(),
        out_specs=vmem(5),
        scratch_shapes=[
            pltpu.VMEM((width, size), BF16),
            pltpu.VMEM((8, width), F32),
            pltpu.SemaphoreType.DMA((2,)),
        ],
        compiler_params=params(32),
        cost_estimate=cost(4 * rows * width * size, 2 * width * size),
    )(meta, levels, counts, normed, weight, modulation, kv)

    parts = pl.pallas_call(
        join_kernel,
        out_shape=(shape((n_head // 2, part, size), BF16),) * 6,
        in_specs=smem(3) + vmem(7),
        out_specs=vmem(6),
        scratch_shapes=[pltpu.VMEM((rows, size), BF16)],
        compiler_params=params(32),
        cost_estimate=cost(4 * rows * width * size, 2 * width * size),
    )(meta, counts, window_mask.T, query, acc, top, total, cross, chip, out_weight)

    pair = shape((2, part, size), BF16)
    small = dict(compiler_params=params(16), cost_estimate=cost(4 * part * size, 8 * part * size))
    ready = []
    for c, (d1, d2, d3) in enumerate(ORDERS):
        keep, give = parts[2 * c : 2 * c + 2]
        got = swap(give, d1)
        keep, give = pl.pallas_call(
            add_kernel, out_shape=(pair, pair), in_specs=vmem(2), out_specs=vmem(2), **small
        )(keep, got)
        got = swap(give, d2)
        keep = pl.pallas_call(
            add_kernel, out_shape=(pair,), in_specs=vmem(2), out_specs=vmem(1), **small
        )(keep, got)[0]
        got = swap(keep, d3)
        fresh = pl.pallas_call(
            functools.partial(update_kernel, c),
            out_shape=pair,
            in_specs=smem() + vmem(4),
            out_specs=vmem()[0],
            **small,
        )(meta, latents, gate, keep, got)
        moved = lax.ppermute(fresh, "queue", [(i, (i - 1) % n_queue) for i in range(n_queue)])
        got = swap(moved, d2)
        four = pl.pallas_call(
            concat_kernel,
            out_shape=shape((4, part, size), BF16),
            in_specs=vmem(2),
            out_specs=vmem()[0],
            **small,
        )(moved, got)
        ready.append((four, swap(four, d1)))

    out = None
    for c, pieces in enumerate(ready):
        out = pl.pallas_call(
            functools.partial(place_kernel, c),
            out_shape=shape((rows, width), BF16),
            in_specs=smem() + hbm(c > 0) + vmem(2),
            out_specs=hbm()[0],
            scratch_shapes=[pltpu.SemaphoreType.DMA((8,))],
            input_output_aliases={1: 0} if c else {},
            **small,
        )(meta, *([out] if c else []), *pieces)
    return out


def solution(mesh):
    in_specs = (P("queue", None), P("queue"), P(), P(), P(), P(None, None, "head"), P("head", None))
    out_specs = P("queue", None)
    return jax.shard_map(body, mesh=mesh, in_specs=in_specs, out_specs=out_specs, check_vma=False)
```

```python
import functools
import math

import jax
import jax.numpy as jnp
from jax import lax
from jax.experimental import pallas as pl
from jax.experimental.pallas import tpu as pltpu
from jax.sharding import PartitionSpec as P

HD = 128
ORDERS = ((4, 1, 3), (1, 3, 4), (3, 4, 1))
CHUNK = 16
LOADS = 3
F32, BF16 = jnp.float32, jnp.bfloat16


def vmem(n=1):
    return [pl.BlockSpec(memory_space=pltpu.VMEM)] * n


def smem(n=1):
    return [pl.BlockSpec(memory_space=pltpu.SMEM)] * n


def hbm(n=1):
    return [pl.BlockSpec(memory_space=pltpu.HBM)] * n


def params(mib):
    return pltpu.CompilerParams(vmem_limit_bytes=mib * 1024 * 1024)


def cost(flops, size):
    return pl.CostEstimate(flops=flops, bytes_accessed=size, transcendentals=0)


def dot(a, b):
    return jnp.dot(a, b, preferred_element_type=F32)


def dot_t(a, b):
    return lax.dot_general(a, b, (((1,), (1,)), ((), ())), preferred_element_type=F32)


def combos(dims):
    found = [0]
    for d in dims:
        found = [f ^ e for f in found for e in (0, d)]
    return found


def columns(target, size):
    return pl.ds(pl.multiple_of(target * size, size), size)


def keys_kernel(level_ref, x_hbm, mod_hbm, w_hbm, kv_ref, q_ref, gate_ref, x_ref, normed_ref, mod_ref, w_ref, sems):
    rows, width = x_ref.shape
    level = level_ref[0]
    first = pl.multiple_of(level // 8 * 8, 8)
    copy_mod = pltpu.make_async_copy(mod_hbm.at[pl.ds(first, 8)], mod_ref, sems.at[0])
    copy_k = pltpu.make_async_copy(w_hbm.at[1], w_ref.at[0], sems.at[1])
    copy_v = pltpu.make_async_copy(w_hbm.at[2], w_ref.at[1], sems.at[2])
    copy_q = pltpu.make_async_copy(w_hbm.at[0], w_ref.at[2], sems.at[3])
    part = rows // LOADS
    copy_x = []
    for i in range(LOADS):
        at = pl.ds(i * part, part)
        copy_x.append(pltpu.make_async_copy(x_hbm.at[at], x_ref.at[at], sems.at[4 + i]))
    copy_mod.start()
    for copy in copy_x:
        copy.start()
    copy_k.start()
    copy_v.start()
    copy_q.start()
    copy_mod.wait()
    row = pl.ds(level % 8, 1)

    def step(i, carry):
        at = pl.ds(pl.multiple_of(i * CHUNK, CHUNK), CHUNK)
        x = x_ref[at, :].astype(F32)
        mean = jnp.mean(x, axis=-1, keepdims=True)
        centered = x - mean
        variance = jnp.mean(centered * centered, axis=-1, keepdims=True)
        scaled = centered * lax.rsqrt(variance + 1e-06)
        normed = scaled * (1.0 + mod_ref[row, width : 2 * width]) + mod_ref[row, :width]
        normed_ref[at, :] = normed.astype(BF16)
        return carry

    steps = part // CHUNK
    for i, copy in enumerate(copy_x):
        copy.wait()
        lax.fori_loop(i * steps, (i + 1) * steps, step, 0, unroll=steps)
    gate_ref[...] = mod_ref[row, 2 * width :]
    copy_k.wait()
    kv_ref[0] = dot(normed_ref[...], w_ref[0]).astype(BF16)
    copy_v.wait()
    kv_ref[1] = dot(normed_ref[...], w_ref[1]).astype(BF16)
    copy_q.wait()
    q_ref[...] = dot(normed_ref[...], w_ref[2]).astype(BF16)


def masked(scores, limit):
    spots = lax.broadcasted_iota(jnp.int32, scores.shape, 1)
    return jnp.where(spots < limit, scores * (1.0 / math.sqrt(HD)), -jnp.inf)


def self_kernel(meta_ref, counts_ref, q_ref, kv_ref, o_ref, m_ref, l_ref):
    rows = q_ref.shape[0]
    limit = counts_ref[meta_ref[0]]
    for head in range(q_ref.shape[1] // HD):
        at = slice(head * HD, (head + 1) * HD)
        scores = masked(dot_t(q_ref[:, at], kv_ref[0, :, at]), limit)
        top = jnp.max(scores, axis=-1, keepdims=True)
        expo = jnp.exp(scores - top)
        m_ref[:, at] = jnp.broadcast_to(top, (rows, HD))
        l_ref[:, at] = jnp.broadcast_to(jnp.sum(expo, axis=-1, keepdims=True), (rows, HD))
        o_ref[:, at] = dot(expo.astype(BF16), kv_ref[1, :, at])


def join_kernel(meta_ref, counts_ref, mask_ref, q_ref, o_ref, m_ref, l_ref, cross_ref, chip_ref, w_ref, *refs):
    outs, att_ref = refs[:-1], refs[-1]
    places = counts_ref.shape[0]
    place, h = meta_ref[0], meta_ref[1]
    before = jnp.where(place > 0, counts_ref[jnp.maximum(place - 1, 0)] * mask_ref[0, place], 0)
    after = jnp.where(
        place < places - 1, counts_ref[jnp.minimum(place + 1, places - 1)] * mask_ref[1, place], 0
    )
    odd = place % 2 == 1
    cross = jnp.where(odd, after, before)
    chip = jnp.where(odd, before, after)
    for head in range(q_ref.shape[1] // HD):
        at = slice(head * HD, (head + 1) * HD)
        query = q_ref[:, at]
        left = masked(dot_t(query, cross_ref[0, :, at]), cross)
        right = masked(dot_t(query, chip_ref[0, :, at]), chip)
        old = m_ref[:, at][:, :1]
        top = jnp.maximum(old, jnp.max(jnp.maximum(left, right), axis=-1, keepdims=True))
        left = jnp.exp(left - top)
        right = jnp.exp(right - top)
        keep = jnp.exp(old - top)
        total = l_ref[:, at][:, :1] * keep + jnp.sum(left + right, axis=-1, keepdims=True)
        acc = o_ref[:, at] * keep
        acc = acc + dot(left.astype(BF16), cross_ref[1, :, at])
        acc = acc + dot(right.astype(BF16), chip_ref[1, :, at])
        att_ref[:, at] = (acc / total).astype(BF16)
    rows, size = q_ref.shape
    part = rows // len(ORDERS)
    for k in range(w_ref.shape[1] // size):
        result = dot(att_ref[...], w_ref[:, columns(h ^ k, size)]).astype(BF16)
        for c, dims in enumerate(ORDERS):
            spot = combos(dims).index(k)
            outs[2 * c + spot // 4][spot % 4] = result[c * part : (c + 1) * part]


def add_kernel(keep_ref, got_ref, *outs):
    total = (keep_ref[...].astype(F32) + got_ref[...].astype(F32)).astype(BF16)
    if len(outs) == 1:
        outs[0][...] = total
    else:
        half = total.shape[0] // 2
        outs[0][...] = total[:half]
        outs[1][...] = total[half:]


def update_kernel(chain, meta_ref, x_ref, gate_ref, keep_ref, got_ref, out_ref):
    part, size = out_ref.shape[1:]
    for c, step in enumerate((0, ORDERS[chain][2])):
        at = columns(meta_ref[1] ^ step, size)
        total = keep_ref[c].astype(F32) + got_ref[1 - c].astype(F32)
        x = x_ref[chain * part : (chain + 1) * part, at].astype(F32)
        out_ref[c] = (x + gate_ref[:, at] * total).astype(BF16)


def concat_kernel(a_ref, b_ref, out_ref):
    half = a_ref.shape[0]
    out_ref[:half] = a_ref[...]
    out_ref[half:] = b_ref[...]


def place_kernel(meta_ref, *refs):
    pieces, out, sems = refs[:-2], refs[-2], refs[-1]
    part, size = pieces[0].shape[1:]
    copies = []
    for c, dims in enumerate(ORDERS):
        for i, step in enumerate(combos(dims)):
            piece = pieces[2 * c + i // 4].at[i % 4]
            to = out.at[pl.ds(c * part, part), columns(meta_ref[1] ^ step, size)]
            copies.append(pltpu.make_async_copy(piece, to, sems.at[len(copies)]))
            copies[-1].start()
    for copy in copies:
        copy.wait()


def body(latents, levels, counts, window_mask, modulation, qkv_weight, out_weight):
    rows, width = latents.shape
    size = qkv_weight.shape[2]
    part = rows // len(ORDERS)
    weight = jnp.transpose(qkv_weight, (1, 0, 2))
    n_head = lax.axis_size("head")
    n_queue = lax.axis_size("queue")
    meta = jnp.stack([lax.axis_index("queue"), lax.axis_index("head")]).astype(jnp.int32)
    shape = jax.ShapeDtypeStruct

    def swap(array, step):
        return lax.ppermute(array, "head", [(i, i ^ step) for i in range(n_head)])

    kv, query, gate = pl.pallas_call(
        keys_kernel,
        out_shape=(shape((2, rows, size), BF16), shape((rows, size), BF16), shape((1, width), F32)),
        in_specs=smem() + hbm(3),
        out_specs=vmem(3),
        scratch_shapes=[
            pltpu.VMEM((rows, width), BF16),
            pltpu.VMEM((rows, width), BF16),
            pltpu.VMEM((8, 3 * width), F32),
            pltpu.VMEM((3, width, size), BF16),
            pltpu.SemaphoreType.DMA((4 + LOADS,)),
        ],
        compiler_params=params(53),
        cost_estimate=cost(4 * rows * width * size, 4 * width * size),
    )(levels, latents, modulation, weight)

    chip = lax.ppermute(kv, "queue", [(i, i ^ 1) for i in range(n_queue)])
    route = []
    for i in range(n_queue):
        j = i - 1 + i % 2 * 2
        for k in range(n_head):
            there = j * n_head + k if 0 <= j < n_queue else i * n_head + (k ^ 1)
            route.append((i * n_head + k, there))
    cross = lax.ppermute(kv, ("queue", "head"), route)

    acc, top, total = pl.pallas_call(
        self_kernel,
        out_shape=(shape((rows, size), F32),) * 3,
        in_specs=smem(2) + vmem(2),
        out_specs=vmem(3),
        compiler_params=params(24),
        cost_estimate=cost(1, 1),
    )(meta, counts, query, kv)

    parts = pl.pallas_call(
        join_kernel,
        out_shape=(shape((n_head // 2, part, size), BF16),) * 6,
        in_specs=smem(3) + vmem(7),
        out_specs=vmem(6),
        scratch_shapes=[pltpu.VMEM((rows, size), BF16)],
        compiler_params=params(32),
        cost_estimate=cost(4 * rows * width * size, 2 * width * size),
    )(meta, counts, window_mask.T, query, acc, top, total, cross, chip, out_weight)

    pair = shape((2, part, size), BF16)
    small = dict(compiler_params=params(16), cost_estimate=cost(4 * part * size, 8 * part * size))
    ready = []
    for c, (d1, d2, d3) in enumerate(ORDERS):
        keep, give = parts[2 * c : 2 * c + 2]
        got = swap(give, d1)
        keep, give = pl.pallas_call(
            add_kernel, out_shape=(pair, pair), in_specs=vmem(2), out_specs=vmem(2), **small
        )(keep, got)
        got = swap(give, d2)
        keep = pl.pallas_call(
            add_kernel, out_shape=(pair,), in_specs=vmem(2), out_specs=vmem(1), **small
        )(keep, got)[0]
        got = swap(keep, d3)
        fresh = pl.pallas_call(
            functools.partial(update_kernel, c),
            out_shape=pair,
            in_specs=smem() + vmem(4),
            out_specs=vmem()[0],
            **small,
        )(meta, latents, gate, keep, got)
        moved = lax.ppermute(fresh, "queue", [(i, (i - 1) % n_queue) for i in range(n_queue)])
        got = swap(moved, d2)
        four = pl.pallas_call(
            concat_kernel,
            out_shape=shape((4, part, size), BF16),
            in_specs=vmem(2),
            out_specs=vmem()[0],
            **small,
        )(moved, got)
        ready += [four, swap(four, d1)]

    return pl.pallas_call(
        place_kernel,
        out_shape=shape((rows, width), BF16),
        in_specs=smem() + vmem(len(ready)),
        out_specs=hbm()[0],
        scratch_shapes=[pltpu.SemaphoreType.DMA((4 * len(ready),))],
        **small,
    )(meta, *ready)


def solution(mesh):
    in_specs = (P("queue", None), P("queue"), P(), P(), P(), P(None, None, "head"), P("head", None))
    out_specs = P("queue", None)
    return jax.shard_map(body, mesh=mesh, in_specs=in_specs, out_specs=out_specs, check_vma=False)
```

```python
import functools
import math

import jax
import jax.numpy as jnp
from jax import lax
from jax.experimental import pallas as pl
from jax.experimental.pallas import tpu as pltpu
from jax.sharding import PartitionSpec as P

HD = 128
ROWS = (96, 96, 96)
ORDERS = ((4, 1, 3), (1, 3, 4), (3, 4, 1))
HALVES = (True, True, True)
GATHER = (False, False, False)
CHUNK = 16
LOADS = 3
NEAR = 48
F32, BF16 = jnp.float32, jnp.bfloat16


def vmem(n=1):
    return [pl.BlockSpec(memory_space=pltpu.VMEM)] * n


def smem(n=1):
    return [pl.BlockSpec(memory_space=pltpu.SMEM)] * n


def hbm(n=1):
    return [pl.BlockSpec(memory_space=pltpu.HBM)] * n


def params(mib):
    return pltpu.CompilerParams(vmem_limit_bytes=mib * 1024 * 1024)


def cost(flops, size):
    return pl.CostEstimate(flops=flops, bytes_accessed=size, transcendentals=0)


def dot(a, b):
    return jnp.dot(a, b, preferred_element_type=F32)


def dot_t(a, b):
    return lax.dot_general(a, b, (((1,), (1,)), ((), ())), preferred_element_type=F32)


def combos(dims):
    found = [0]
    for d in dims:
        found = [f ^ e for f in found for e in (0, d)]
    return found


def rows_of(chain):
    start = sum(ROWS[:chain])
    return slice(start, start + ROWS[chain])


def columns(target, size):
    return pl.ds(pl.multiple_of(target * size, size), size)


def load(pieces, target, sems, first):
    part = target.shape[0] // LOADS
    copies = []
    for i in range(LOADS):
        at = pl.ds(i * part, part)
        copies.append(pltpu.make_async_copy(pieces.at[at], target.at[at], sems.at[first + i]))
        copies[-1].start()
    return copies


def normalize(copies, x_ref, mod_ref, row, normed_ref):
    rows, width = x_ref.shape

    def step(i, carry):
        at = pl.ds(pl.multiple_of(i * CHUNK, CHUNK), CHUNK)
        x = x_ref[at, :].astype(F32)
        mean = jnp.mean(x, axis=-1, keepdims=True)
        centered = x - mean
        variance = jnp.mean(centered * centered, axis=-1, keepdims=True)
        scaled = centered * lax.rsqrt(variance + 1e-06)
        normed = scaled * (1.0 + mod_ref[row, width : 2 * width]) + mod_ref[row, :width]
        normed_ref[at, :] = normed.astype(BF16)
        return carry

    steps = rows // LOADS // CHUNK
    for i, copy in enumerate(copies):
        copy.wait()
        lax.fori_loop(i * steps, (i + 1) * steps, step, 0, unroll=steps)


def keys_kernel(level_ref, x_hbm, mod_hbm, w_hbm, kv_ref, table_ref, x_ref, normed_ref, mod_ref, w_ref, sems):
    level = level_ref[0]
    first = pl.multiple_of(level // 8 * 8, 8)
    copy_mod = pltpu.make_async_copy(mod_hbm.at[pl.ds(first, 8)], mod_ref, sems.at[0])
    copy_k = pltpu.make_async_copy(w_hbm.at[1], w_ref.at[0], sems.at[1])
    copy_v = pltpu.make_async_copy(w_hbm.at[2], w_ref.at[1], sems.at[2])
    copy_mod.start()
    copies = load(x_hbm, x_ref, sems, 3)
    copy_k.start()
    copy_v.start()
    copy_mod.wait()
    row = pl.ds(level % 8, 1)
    normalize(copies, x_ref, mod_ref, row, normed_ref)
    table_ref[...] = mod_ref[row, :]
    copy_k.wait()
    kv_ref[0] = dot(normed_ref[...], w_ref[0]).astype(BF16)
    copy_v.wait()
    kv_ref[1] = dot(normed_ref[...], w_ref[1]).astype(BF16)


def masked(scores, limit):
    spots = lax.broadcasted_iota(jnp.int32, scores.shape, 1)
    return jnp.where(spots < limit, scores * (1.0 / math.sqrt(HD)), -jnp.inf)


def limits(place, counts_ref, mask_ref):
    places = counts_ref.shape[0]
    before = jnp.where(place > 0, counts_ref[jnp.maximum(place - 1, 0)] * mask_ref[0, place], 0)
    after = jnp.where(
        place < places - 1, counts_ref[jnp.minimum(place + 1, places - 1)] * mask_ref[1, place], 0
    )
    odd = place % 2 == 1
    return jnp.where(odd, before, after), jnp.where(odd, after, before)


def near_kernel(
    meta_ref, counts_ref, mask_ref, x_hbm, table_ref, w_hbm, kv_ref, chip_ref, q_ref, o_ref, m_ref, l_ref, *scratch
):
    x_ref, normed_ref, w_ref, sems = scratch
    rows, size = q_ref.shape
    copies = load(x_hbm, x_ref, sems, 1)
    copy_q = pltpu.make_async_copy(w_hbm.at[0], w_ref, sems.at[0])
    copy_q.start()
    normalize(copies, x_ref, table_ref, slice(0, 1), normed_ref)
    copy_q.wait()
    q_ref[...] = dot(normed_ref[...], w_ref[...]).astype(BF16)
    place = meta_ref[0]
    own = counts_ref[place]
    chip = limits(place, counts_ref, mask_ref)[0]
    for head in range(size // HD):
        at = slice(head * HD, (head + 1) * HD)
        query = q_ref[:, at]
        left = masked(dot_t(query, kv_ref[0, :, at]), own)
        right = masked(dot_t(query, chip_ref[0, :, at]), chip)
        top = jnp.max(jnp.maximum(left, right), axis=-1, keepdims=True)
        left = jnp.exp(left - top)
        right = jnp.exp(right - top)
        m_ref[:, at] = jnp.broadcast_to(top, (rows, HD))
        l_ref[:, at] = jnp.broadcast_to(jnp.sum(left + right, axis=-1, keepdims=True), (rows, HD))
        o_ref[:, at] = dot(left.astype(BF16), kv_ref[1, :, at]) + dot(right.astype(BF16), chip_ref[1, :, at])


def join_kernel(meta_ref, counts_ref, mask_ref, q_ref, o_ref, m_ref, l_ref, far_ref, w_ref, *refs):
    outs, att_ref = refs[:-1], refs[-1]
    h = meta_ref[1]
    limit = limits(meta_ref[0], counts_ref, mask_ref)[1]
    rows, size = q_ref.shape
    for head in range(size // HD):
        at = slice(head * HD, (head + 1) * HD)
        scores = masked(dot_t(q_ref[:, at], far_ref[0, :, at]), limit)
        old = m_ref[:, at][:, :1]
        top = jnp.maximum(old, jnp.max(scores, axis=-1, keepdims=True))
        expo = jnp.exp(scores - top)
        keep = jnp.exp(old - top)
        total = l_ref[:, at][:, :1] * keep + jnp.sum(expo, axis=-1, keepdims=True)
        acc = o_ref[:, at] * keep + dot(expo.astype(BF16), far_ref[1, :, at])
        att_ref[:, at] = (acc / total).astype(BF16)
    for k in range(w_ref.shape[1] // size):
        result = dot(att_ref[...], w_ref[:, columns(h ^ k, size)]).astype(BF16)
        first = 0
        for c, dims in enumerate(ORDERS):
            spot = combos(dims).index(k)
            held = outs[first].shape[0]
            outs[first + spot // held][spot % held] = result[rows_of(c)]
            first += 8 // held


def add_kernel(starts, *refs):
    total = 0.0
    for start, ref in zip(starts, refs):
        total = total + ref[start : start + 2].astype(F32)
    refs[-1][...] = total.astype(BF16)


def update_kernel(chain, meta_ref, x_ref, table_ref, keep_ref, got_ref, out_ref):
    size = out_ref.shape[2]
    n_head = x_ref.shape[1] // size
    for j in range(2):
        target = meta_ref[1] ^ combos(ORDERS[chain])[j]
        at = columns(target, size)
        total = keep_ref[j].astype(F32) + got_ref[1 - j].astype(F32)
        x = x_ref[rows_of(chain), at].astype(F32)
        out_ref[j] = (x + table_ref[:, columns(2 * n_head + target, size)] * total).astype(BF16)


def concat_kernel(a_ref, b_ref, out_ref):
    half = a_ref.shape[0]
    out_ref[:half] = a_ref[...]
    out_ref[half:] = b_ref[...]


def place_kernel(meta_ref, *refs):
    pieces, out, sems = refs[:-2], refs[-2], refs[-1]
    size = pieces[0].shape[2]
    copies = []
    first = 0
    for c, part in enumerate(ROWS):
        held = pieces[first].shape[0]
        for spot in range(8):
            piece = pieces[first + spot // held].at[spot % held]
            target = meta_ref[1] ^ combos(ORDERS[c])[spot]
            to = out.at[pl.ds(rows_of(c).start, part), columns(target, size)]
            copies.append(pltpu.make_async_copy(piece, to, sems.at[len(copies)]))
            copies[-1].start()
        first += 8 // held
    for copy in copies:
        copy.wait()


def body(latents, levels, counts, window_mask, modulation, qkv_weight, out_weight):
    rows, width = latents.shape
    size = qkv_weight.shape[2]
    weight = jnp.transpose(qkv_weight, (1, 0, 2))
    n_head = lax.axis_size("head")
    n_queue = lax.axis_size("queue")
    meta = jnp.stack([lax.axis_index("queue"), lax.axis_index("head")]).astype(jnp.int32)
    shape = jax.ShapeDtypeStruct

    def swap(array, chain, level):
        step = ORDERS[chain][level]
        return lax.ppermute(array, "head", [(i, i ^ step) for i in range(n_head)])

    kv, table = pl.pallas_call(
        keys_kernel,
        out_shape=(shape((2, rows, size), BF16), shape((1, 3 * width), F32)),
        in_specs=smem() + hbm(3),
        out_specs=vmem(2),
        scratch_shapes=[
            pltpu.VMEM((rows, width), BF16),
            pltpu.VMEM((rows, width), BF16),
            pltpu.VMEM((8, 3 * width), F32),
            pltpu.VMEM((2, width, size), BF16),
            pltpu.SemaphoreType.DMA((3 + LOADS,)),
        ],
        compiler_params=params(53),
        cost_estimate=cost(4 * rows * width * size, 4 * width * size),
    )(levels, latents, modulation, weight)

    chip = lax.ppermute(kv, "queue", [(i, i ^ 1) for i in range(n_queue)])
    route = []
    for i in range(n_queue):
        j = i - 1 + i % 2 * 2
        for k in range(n_head):
            there = j * n_head + k if 0 <= j < n_queue else i * n_head + (k ^ 1)
            route.append((i * n_head + k, there))
    cross = lax.ppermute(kv, ("queue", "head"), route)

    query, *state = pl.pallas_call(
        near_kernel,
        out_shape=(shape((rows, size), BF16),) + (shape((rows, size), F32),) * 3,
        in_specs=smem(3) + hbm() + vmem() + hbm() + vmem(2),
        out_specs=vmem(4),
        scratch_shapes=[
            pltpu.VMEM((rows, width), BF16),
            pltpu.VMEM((rows, width), BF16),
            pltpu.VMEM((width, size), BF16),
            pltpu.SemaphoreType.DMA((1 + LOADS,)),
        ],
        compiler_params=params(NEAR),
        cost_estimate=cost(1, 1),
    )(meta, counts, window_mask.T, latents, table, weight, kv, chip)

    held = [2 if half else 4 for half in HALVES]
    parts = pl.pallas_call(
        join_kernel,
        out_shape=tuple(shape((n, part, size), BF16) for n, part in zip(held, ROWS) for _ in range(8 // n)),
        in_specs=smem(3) + vmem(6),
        out_specs=(vmem()[0],) * sum(8 // n for n in held),
        scratch_shapes=[pltpu.VMEM((rows, size), BF16)],
        compiler_params=params(32),
        cost_estimate=cost(4 * rows * width * size, 2 * width * size),
    )(meta, counts, window_mask.T, query, *state, cross, out_weight)

    small = dict(compiler_params=params(16), cost_estimate=cost(4 * 96 * size, 8 * 96 * size))

    def add(part, *terms):
        return pl.pallas_call(
            functools.partial(add_kernel, [start for start, _ in terms]),
            out_shape=shape((2, part, size), BF16),
            in_specs=vmem(len(terms)),
            out_specs=vmem()[0],
            **small,
        )(*[term for _, term in terms])

    chains = range(len(ROWS))
    keep, pass_on, got, got_on = {}, {}, {}, {}
    for c in chains:
        if HALVES[c]:
            keep[c], pass_on[c], give, give_on = parts[:4]
            parts = parts[4:]
            got_on[c] = swap(give_on, c, 0)
            got[c] = swap(give, c, 0)
        else:
            keep[c], give = parts[:2]
            parts = parts[2:]
            got[c] = swap(give, c, 0)
    relayed = {}
    for c, part in enumerate(ROWS):
        if HALVES[c]:
            term = add(part, (0, pass_on[c]), (0, got_on[c]))
        else:
            term = add(part, (2, keep[c]), (2, got[c]))
        relayed[c] = swap(term, c, 1)
    mine, other = {}, {}
    for c, part in enumerate(ROWS):
        mine[c] = add(part, (0, keep[c]), (0, got[c]), (0, relayed[c]))
        other[c] = swap(mine[c], c, 2)
    moved = {}
    for c, part in enumerate(ROWS):
        fresh = pl.pallas_call(
            functools.partial(update_kernel, c),
            out_shape=shape((2, part, size), BF16),
            in_specs=smem() + vmem(4),
            out_specs=vmem()[0],
            **small,
        )(meta, latents, table, mine[c], other[c])
        moved[c] = lax.ppermute(fresh, "queue", [(i, (i - 1) % n_queue) for i in range(n_queue)])
    ready = []
    for c, part in enumerate(ROWS):
        near = swap(moved[c], c, 1)
        if GATHER[c]:
            ready += [moved[c], near, swap(moved[c], c, 0), swap(near, c, 0)]
        else:
            four = pl.pallas_call(
                concat_kernel,
                out_shape=shape((4, part, size), BF16),
                in_specs=vmem(2),
                out_specs=vmem()[0],
                **small,
            )(moved[c], near)
            ready += [four, swap(four, c, 0)]

    return pl.pallas_call(
        place_kernel,
        out_shape=shape((rows, width), BF16),
        in_specs=smem() + vmem(len(ready)),
        out_specs=hbm()[0],
        scratch_shapes=[pltpu.SemaphoreType.DMA((8 * len(ROWS),))],
        **small,
    )(meta, *ready)


def solution(mesh):
    in_specs = (P("queue", None), P("queue"), P(), P(), P(), P(None, None, "head"), P("head", None))
    out_specs = P("queue", None)
    return jax.shard_map(body, mesh=mesh, in_specs=in_specs, out_specs=out_specs, check_vma=False)
```

```python
import functools
import math

import jax
import jax.numpy as jnp
from jax import lax
from jax.experimental import pallas as pl
from jax.experimental.pallas import tpu as pltpu
from jax.sharding import PartitionSpec as P

HD = 128
ROWS = (96, 96, 96)
ORDERS = ((1, 4, 3), (3, 1, 4), (4, 3, 1))
HALVES = (True, True, True)
GATHER = (False, False, False)
CHUNK = 16
LOADS = 3
NEAR = 48
F32, BF16 = jnp.float32, jnp.bfloat16


def vmem(n=1):
    return [pl.BlockSpec(memory_space=pltpu.VMEM)] * n


def smem(n=1):
    return [pl.BlockSpec(memory_space=pltpu.SMEM)] * n


def hbm(n=1):
    return [pl.BlockSpec(memory_space=pltpu.HBM)] * n


def params(mib):
    return pltpu.CompilerParams(vmem_limit_bytes=mib * 1024 * 1024)


def cost(flops, size):
    return pl.CostEstimate(flops=flops, bytes_accessed=size, transcendentals=0)


def dot(a, b):
    return jnp.dot(a, b, preferred_element_type=F32)


def dot_t(a, b):
    return lax.dot_general(a, b, (((1,), (1,)), ((), ())), preferred_element_type=F32)


def combos(dims):
    found = [0]
    for d in dims:
        found = [f ^ e for f in found for e in (0, d)]
    return found


def rows_of(chain):
    start = sum(ROWS[:chain])
    return slice(start, start + ROWS[chain])


def columns(target, size):
    return pl.ds(pl.multiple_of(target * size, size), size)


def load(pieces, target, sems, first):
    part = target.shape[0] // LOADS
    copies = []
    for i in range(LOADS):
        at = pl.ds(i * part, part)
        copies.append(pltpu.make_async_copy(pieces.at[at], target.at[at], sems.at[first + i]))
        copies[-1].start()
    return copies


def normalize(copies, x_ref, mod_ref, row, normed_ref):
    rows, width = x_ref.shape

    def step(i, carry):
        at = pl.ds(pl.multiple_of(i * CHUNK, CHUNK), CHUNK)
        x = x_ref[at, :].astype(F32)
        mean = jnp.mean(x, axis=-1, keepdims=True)
        centered = x - mean
        variance = jnp.mean(centered * centered, axis=-1, keepdims=True)
        scaled = centered * lax.rsqrt(variance + 1e-06)
        normed = scaled * (1.0 + mod_ref[row, width : 2 * width]) + mod_ref[row, :width]
        normed_ref[at, :] = normed.astype(BF16)
        return carry

    steps = rows // LOADS // CHUNK
    for i, copy in enumerate(copies):
        copy.wait()
        lax.fori_loop(i * steps, (i + 1) * steps, step, 0, unroll=steps)


def keys_kernel(level_ref, x_hbm, mod_hbm, w_hbm, kv_ref, table_ref, x_ref, normed_ref, mod_ref, w_ref, sems):
    level = level_ref[0]
    first = pl.multiple_of(level // 8 * 8, 8)
    copy_mod = pltpu.make_async_copy(mod_hbm.at[pl.ds(first, 8)], mod_ref, sems.at[0])
    copy_k = pltpu.make_async_copy(w_hbm.at[1], w_ref.at[0], sems.at[1])
    copy_v = pltpu.make_async_copy(w_hbm.at[2], w_ref.at[1], sems.at[2])
    copy_mod.start()
    copies = load(x_hbm, x_ref, sems, 3)
    copy_k.start()
    copy_v.start()
    copy_mod.wait()
    row = pl.ds(level % 8, 1)
    normalize(copies, x_ref, mod_ref, row, normed_ref)
    table_ref[...] = mod_ref[row, :]
    copy_k.wait()
    kv_ref[0] = dot(normed_ref[...], w_ref[0]).astype(BF16)
    copy_v.wait()
    kv_ref[1] = dot(normed_ref[...], w_ref[1]).astype(BF16)


def masked(scores, limit):
    spots = lax.broadcasted_iota(jnp.int32, scores.shape, 1)
    return jnp.where(spots < limit, scores * (1.0 / math.sqrt(HD)), -jnp.inf)


def limits(place, counts_ref, mask_ref):
    places = counts_ref.shape[0]
    before = jnp.where(place > 0, counts_ref[jnp.maximum(place - 1, 0)] * mask_ref[0, place], 0)
    after = jnp.where(
        place < places - 1, counts_ref[jnp.minimum(place + 1, places - 1)] * mask_ref[1, place], 0
    )
    odd = place % 2 == 1
    return jnp.where(odd, before, after), jnp.where(odd, after, before)


def near_kernel(
    meta_ref, counts_ref, mask_ref, x_hbm, table_ref, w_hbm, kv_ref, chip_ref, q_ref, o_ref, m_ref, l_ref, *scratch
):
    x_ref, normed_ref, w_ref, sems = scratch
    rows, size = q_ref.shape
    copies = load(x_hbm, x_ref, sems, 1)
    copy_q = pltpu.make_async_copy(w_hbm.at[0], w_ref, sems.at[0])
    copy_q.start()
    normalize(copies, x_ref, table_ref, slice(0, 1), normed_ref)
    copy_q.wait()
    q_ref[...] = dot(normed_ref[...], w_ref[...]).astype(BF16)
    place = meta_ref[0]
    own = counts_ref[place]
    chip = limits(place, counts_ref, mask_ref)[0]
    for head in range(size // HD):
        at = slice(head * HD, (head + 1) * HD)
        query = q_ref[:, at]
        left = masked(dot_t(query, kv_ref[0, :, at]), own)
        right = masked(dot_t(query, chip_ref[0, :, at]), chip)
        top = jnp.max(jnp.maximum(left, right), axis=-1, keepdims=True)
        left = jnp.exp(left - top)
        right = jnp.exp(right - top)
        m_ref[:, at] = jnp.broadcast_to(top, (rows, HD))
        l_ref[:, at] = jnp.broadcast_to(jnp.sum(left + right, axis=-1, keepdims=True), (rows, HD))
        o_ref[:, at] = dot(left.astype(BF16), kv_ref[1, :, at]) + dot(right.astype(BF16), chip_ref[1, :, at])


def join_kernel(meta_ref, counts_ref, mask_ref, q_ref, o_ref, m_ref, l_ref, far_ref, w_ref, *refs):
    outs, att_ref = refs[:-1], refs[-1]
    h = meta_ref[1]
    limit = limits(meta_ref[0], counts_ref, mask_ref)[1]
    rows, size = q_ref.shape
    for head in range(size // HD):
        at = slice(head * HD, (head + 1) * HD)
        scores = masked(dot_t(q_ref[:, at], far_ref[0, :, at]), limit)
        old = m_ref[:, at][:, :1]
        top = jnp.maximum(old, jnp.max(scores, axis=-1, keepdims=True))
        expo = jnp.exp(scores - top)
        keep = jnp.exp(old - top)
        total = l_ref[:, at][:, :1] * keep + jnp.sum(expo, axis=-1, keepdims=True)
        acc = o_ref[:, at] * keep + dot(expo.astype(BF16), far_ref[1, :, at])
        att_ref[:, at] = (acc / total).astype(BF16)
    for k in range(w_ref.shape[1] // size):
        result = dot(att_ref[...], w_ref[:, columns(h ^ k, size)]).astype(BF16)
        first = 0
        for c, dims in enumerate(ORDERS):
            spot = combos(dims).index(k)
            held = outs[first].shape[0]
            outs[first + spot // held][spot % held] = result[rows_of(c)]
            first += 8 // held


def add_kernel(starts, *refs):
    total = 0.0
    for start, ref in zip(starts, refs):
        total = total + ref[start : start + 2].astype(F32)
    refs[-1][...] = total.astype(BF16)


def update_kernel(chain, meta_ref, x_ref, table_ref, keep_ref, got_ref, out_ref):
    size = out_ref.shape[2]
    n_head = x_ref.shape[1] // size
    for j in range(2):
        target = meta_ref[1] ^ combos(ORDERS[chain])[j]
        at = columns(target, size)
        total = keep_ref[j].astype(F32) + got_ref[1 - j].astype(F32)
        x = x_ref[rows_of(chain), at].astype(F32)
        out_ref[j] = (x + table_ref[:, columns(2 * n_head + target, size)] * total).astype(BF16)


def concat_kernel(a_ref, b_ref, out_ref):
    half = a_ref.shape[0]
    out_ref[:half] = a_ref[...]
    out_ref[half:] = b_ref[...]


def place_kernel(chains, meta_ref, *refs):
    pieces, out, sems = refs[-2 - 2 * len(chains) : -2], refs[-2], refs[-1]
    size = pieces[0].shape[2]
    copies = []
    for i, c in enumerate(chains):
        for spot, step in enumerate(combos(ORDERS[c])):
            piece = pieces[2 * i + spot // 4].at[spot % 4]
            to = out.at[pl.ds(rows_of(c).start, ROWS[c]), columns(meta_ref[1] ^ step, size)]
            copies.append(pltpu.make_async_copy(piece, to, sems.at[len(copies)]))
            copies[-1].start()
    for copy in copies:
        copy.wait()


def body(latents, levels, counts, window_mask, modulation, qkv_weight, out_weight):
    rows, width = latents.shape
    size = qkv_weight.shape[2]
    weight = jnp.transpose(qkv_weight, (1, 0, 2))
    n_head = lax.axis_size("head")
    n_queue = lax.axis_size("queue")
    meta = jnp.stack([lax.axis_index("queue"), lax.axis_index("head")]).astype(jnp.int32)
    shape = jax.ShapeDtypeStruct

    def swap(array, chain, level):
        step = ORDERS[chain][level]
        return lax.ppermute(array, "head", [(i, i ^ step) for i in range(n_head)])

    kv, table = pl.pallas_call(
        keys_kernel,
        out_shape=(shape((2, rows, size), BF16), shape((1, 3 * width), F32)),
        in_specs=smem() + hbm(3),
        out_specs=vmem(2),
        scratch_shapes=[
            pltpu.VMEM((rows, width), BF16),
            pltpu.VMEM((rows, width), BF16),
            pltpu.VMEM((8, 3 * width), F32),
            pltpu.VMEM((2, width, size), BF16),
            pltpu.SemaphoreType.DMA((3 + LOADS,)),
        ],
        compiler_params=params(53),
        cost_estimate=cost(4 * rows * width * size, 4 * width * size),
    )(levels, latents, modulation, weight)

    chip = lax.ppermute(kv, "queue", [(i, i ^ 1) for i in range(n_queue)])
    route = []
    for i in range(n_queue):
        j = i - 1 + i % 2 * 2
        for k in range(n_head):
            there = j * n_head + k if 0 <= j < n_queue else i * n_head + (k ^ 1)
            route.append((i * n_head + k, there))
    cross = lax.ppermute(kv, ("queue", "head"), route)

    query, *state = pl.pallas_call(
        near_kernel,
        out_shape=(shape((rows, size), BF16),) + (shape((rows, size), F32),) * 3,
        in_specs=smem(3) + hbm() + vmem() + hbm() + vmem(2),
        out_specs=vmem(4),
        scratch_shapes=[
            pltpu.VMEM((rows, width), BF16),
            pltpu.VMEM((rows, width), BF16),
            pltpu.VMEM((width, size), BF16),
            pltpu.SemaphoreType.DMA((1 + LOADS,)),
        ],
        compiler_params=params(NEAR),
        cost_estimate=cost(1, 1),
    )(meta, counts, window_mask.T, latents, table, weight, kv, chip)

    held = [2 if half else 4 for half in HALVES]
    parts = pl.pallas_call(
        join_kernel,
        out_shape=tuple(shape((n, part, size), BF16) for n, part in zip(held, ROWS) for _ in range(8 // n)),
        in_specs=smem(3) + vmem(6),
        out_specs=(vmem()[0],) * sum(8 // n for n in held),
        scratch_shapes=[pltpu.VMEM((rows, size), BF16)],
        compiler_params=params(32),
        cost_estimate=cost(4 * rows * width * size, 2 * width * size),
    )(meta, counts, window_mask.T, query, *state, cross, out_weight)

    small = dict(compiler_params=params(16), cost_estimate=cost(4 * 96 * size, 8 * 96 * size))

    def add(part, *terms):
        return pl.pallas_call(
            functools.partial(add_kernel, [start for start, _ in terms]),
            out_shape=shape((2, part, size), BF16),
            in_specs=vmem(len(terms)),
            out_specs=vmem()[0],
            **small,
        )(*[term for _, term in terms])

    chains = range(len(ROWS))
    keep, pass_on, got, got_on = {}, {}, {}, {}
    for c in chains:
        if HALVES[c]:
            keep[c], pass_on[c], give, give_on = parts[:4]
            parts = parts[4:]
            got_on[c] = swap(give_on, c, 0)
            got[c] = swap(give, c, 0)
        else:
            keep[c], give = parts[:2]
            parts = parts[2:]
            got[c] = swap(give, c, 0)
    relayed = {}
    for c, part in enumerate(ROWS):
        if HALVES[c]:
            term = add(part, (0, pass_on[c]), (0, got_on[c]))
        else:
            term = add(part, (2, keep[c]), (2, got[c]))
        relayed[c] = swap(term, c, 1)
    mine, other = {}, {}
    for c, part in enumerate(ROWS):
        mine[c] = add(part, (0, keep[c]), (0, got[c]), (0, relayed[c]))
        other[c] = swap(mine[c], c, 2)
    moved = {}
    for c, part in enumerate(ROWS):
        fresh = pl.pallas_call(
            functools.partial(update_kernel, c),
            out_shape=shape((2, part, size), BF16),
            in_specs=smem() + vmem(4),
            out_specs=vmem()[0],
            **small,
        )(meta, latents, table, mine[c], other[c])
        moved[c] = lax.ppermute(fresh, "queue", [(i, (i - 1) % n_queue) for i in range(n_queue)])
    ready = []
    for c, part in enumerate(ROWS):
        near = swap(moved[c], c, 1)
        if GATHER[c]:
            ready += [moved[c], near, swap(moved[c], c, 0), swap(near, c, 0)]
        else:
            four = pl.pallas_call(
                concat_kernel,
                out_shape=shape((4, part, size), BF16),
                in_specs=vmem(2),
                out_specs=vmem()[0],
                **small,
            )(moved[c], near)
            ready += [four, swap(four, c, 0)]

    out = []
    for chains in ((0, 1), (2,)):
        out = [
            pl.pallas_call(
                functools.partial(place_kernel, chains),
                out_shape=shape((rows, width), BF16),
                in_specs=smem() + hbm(len(out)) + vmem(2 * len(chains)),
                out_specs=hbm()[0],
                scratch_shapes=[pltpu.SemaphoreType.DMA((8 * len(chains),))],
                input_output_aliases={1: 0} if out else {},
                **small,
            )(meta, *out, *ready[2 * chains[0] : 2 * chains[-1] + 2])
        ]
    return out[0]


def solution(mesh):
    in_specs = (P("queue", None), P("queue"), P(), P(), P(), P(None, None, "head"), P("head", None))
    out_specs = P("queue", None)
    return jax.shard_map(body, mesh=mesh, in_specs=in_specs, out_specs=out_specs, check_vma=False)
```

```python
import functools
import math

import jax
import jax.numpy as jnp
from jax import lax
from jax.experimental import pallas as pl
from jax.experimental.pallas import tpu as pltpu
from jax.sharding import PartitionSpec as P

HD = 128
ROWS = (96, 96, 96)
ORDERS = ((1, 4, 3), (3, 1, 4), (4, 3, 1))
HALVES = (True, True, True)
GATHER = (False, False, False)
CHUNK = 16
LOADS = 3
NEAR = 48
F32, BF16 = jnp.float32, jnp.bfloat16


def vmem(n=1):
    return [pl.BlockSpec(memory_space=pltpu.VMEM)] * n


def smem(n=1):
    return [pl.BlockSpec(memory_space=pltpu.SMEM)] * n


def hbm(n=1):
    return [pl.BlockSpec(memory_space=pltpu.HBM)] * n


def params(mib):
    return pltpu.CompilerParams(vmem_limit_bytes=mib * 1024 * 1024)


def cost(flops, size):
    return pl.CostEstimate(flops=flops, bytes_accessed=size, transcendentals=0)


def dot(a, b):
    return jnp.dot(a, b, preferred_element_type=F32)


def dot_t(a, b):
    return lax.dot_general(a, b, (((1,), (1,)), ((), ())), preferred_element_type=F32)


def combos(dims):
    found = [0]
    for d in dims:
        found = [f ^ e for f in found for e in (0, d)]
    return found


def rows_of(chain):
    start = sum(ROWS[:chain])
    return slice(start, start + ROWS[chain])


def columns(target, size):
    return pl.ds(pl.multiple_of(target * size, size), size)


def load(pieces, target, sems, first):
    part = target.shape[0] // LOADS
    copies = []
    for i in range(LOADS):
        at = pl.ds(i * part, part)
        copies.append(pltpu.make_async_copy(pieces.at[at], target.at[at], sems.at[first + i]))
        copies[-1].start()
    return copies


def normalize(copies, x_ref, mod_ref, row, normed_ref):
    rows, width = x_ref.shape

    def step(i, carry):
        at = pl.ds(pl.multiple_of(i * CHUNK, CHUNK), CHUNK)
        x = x_ref[at, :].astype(F32)
        mean = jnp.mean(x, axis=-1, keepdims=True)
        centered = x - mean
        variance = jnp.mean(centered * centered, axis=-1, keepdims=True)
        scaled = centered * lax.rsqrt(variance + 1e-06)
        normed = scaled * (1.0 + mod_ref[row, width : 2 * width]) + mod_ref[row, :width]
        normed_ref[at, :] = normed.astype(BF16)
        return carry

    steps = rows // LOADS // CHUNK
    for i, copy in enumerate(copies):
        copy.wait()
        lax.fori_loop(i * steps, (i + 1) * steps, step, 0, unroll=steps)


def keys_kernel(level_ref, x_hbm, mod_hbm, w_hbm, kv_ref, table_ref, x_ref, normed_ref, mod_ref, w_ref, sems):
    level = level_ref[0]
    first = pl.multiple_of(level // 8 * 8, 8)
    copy_mod = pltpu.make_async_copy(mod_hbm.at[pl.ds(first, 8)], mod_ref, sems.at[0])
    copy_k = pltpu.make_async_copy(w_hbm.at[1], w_ref.at[0], sems.at[1])
    copy_v = pltpu.make_async_copy(w_hbm.at[2], w_ref.at[1], sems.at[2])
    copy_mod.start()
    copies = load(x_hbm, x_ref, sems, 3)
    copy_k.start()
    copy_v.start()
    copy_mod.wait()
    row = pl.ds(level % 8, 1)
    normalize(copies, x_ref, mod_ref, row, normed_ref)
    table_ref[...] = mod_ref[row, :]
    copy_k.wait()
    kv_ref[0] = dot(normed_ref[...], w_ref[0]).astype(BF16)
    copy_v.wait()
    kv_ref[1] = dot(normed_ref[...], w_ref[1]).astype(BF16)


def masked(scores, limit):
    spots = lax.broadcasted_iota(jnp.int32, scores.shape, 1)
    return jnp.where(spots < limit, scores * (1.0 / math.sqrt(HD)), -jnp.inf)


def limits(place, counts_ref, mask_ref):
    places = counts_ref.shape[0]
    before = jnp.where(place > 0, counts_ref[jnp.maximum(place - 1, 0)] * mask_ref[0, place], 0)
    after = jnp.where(
        place < places - 1, counts_ref[jnp.minimum(place + 1, places - 1)] * mask_ref[1, place], 0
    )
    odd = place % 2 == 1
    return jnp.where(odd, before, after), jnp.where(odd, after, before)


def near_kernel(
    meta_ref, counts_ref, mask_ref, x_hbm, table_ref, w_hbm, kv_ref, chip_ref, q_ref, o_ref, m_ref, l_ref, *scratch
):
    x_ref, normed_ref, w_ref, sems = scratch
    rows, size = q_ref.shape
    copies = load(x_hbm, x_ref, sems, 1)
    copy_q = pltpu.make_async_copy(w_hbm.at[0], w_ref, sems.at[0])
    copy_q.start()
    normalize(copies, x_ref, table_ref, slice(0, 1), normed_ref)
    copy_q.wait()
    q_ref[...] = dot(normed_ref[...], w_ref[...]).astype(BF16)
    place = meta_ref[0]
    own = counts_ref[place]
    chip = limits(place, counts_ref, mask_ref)[0]
    for head in range(size // HD):
        at = slice(head * HD, (head + 1) * HD)
        query = q_ref[:, at]
        left = masked(dot_t(query, kv_ref[0, :, at]), own)
        right = masked(dot_t(query, chip_ref[0, :, at]), chip)
        top = jnp.max(jnp.maximum(left, right), axis=-1, keepdims=True)
        left = jnp.exp(left - top)
        right = jnp.exp(right - top)
        m_ref[:, at] = jnp.broadcast_to(top, (rows, HD))
        l_ref[:, at] = jnp.broadcast_to(jnp.sum(left + right, axis=-1, keepdims=True), (rows, HD))
        o_ref[:, at] = dot(left.astype(BF16), kv_ref[1, :, at]) + dot(right.astype(BF16), chip_ref[1, :, at])


def join_kernel(meta_ref, counts_ref, mask_ref, q_ref, o_ref, m_ref, l_ref, far_ref, w_ref, *refs):
    outs, att_ref = refs[:-1], refs[-1]
    h = meta_ref[1]
    limit = limits(meta_ref[0], counts_ref, mask_ref)[1]
    rows, size = q_ref.shape
    for head in range(size // HD):
        at = slice(head * HD, (head + 1) * HD)
        scores = masked(dot_t(q_ref[:, at], far_ref[0, :, at]), limit)
        old = m_ref[:, at][:, :1]
        top = jnp.maximum(old, jnp.max(scores, axis=-1, keepdims=True))
        expo = jnp.exp(scores - top)
        keep = jnp.exp(old - top)
        total = l_ref[:, at][:, :1] * keep + jnp.sum(expo, axis=-1, keepdims=True)
        acc = o_ref[:, at] * keep + dot(expo.astype(BF16), far_ref[1, :, at])
        att_ref[:, at] = (acc / total).astype(BF16)
    for k in range(w_ref.shape[1] // size):
        result = dot(att_ref[...], w_ref[:, columns(h ^ k, size)]).astype(BF16)
        first = 0
        for c, dims in enumerate(ORDERS):
            spot = combos(dims).index(k)
            held = outs[first].shape[0]
            outs[first + spot // held][spot % held] = result[rows_of(c)]
            first += 8 // held


def add_kernel(starts, *refs):
    total = 0.0
    for start, ref in zip(starts, refs):
        total = total + ref[start : start + 2].astype(F32)
    refs[-1][...] = total.astype(BF16)


def update_kernel(chain, meta_ref, x_ref, table_ref, keep_ref, got_ref, out_ref):
    size = out_ref.shape[2]
    n_head = x_ref.shape[1] // size
    for j in range(2):
        target = meta_ref[1] ^ combos(ORDERS[chain])[j]
        at = columns(target, size)
        total = keep_ref[j].astype(F32) + got_ref[1 - j].astype(F32)
        x = x_ref[rows_of(chain), at].astype(F32)
        out_ref[j] = (x + table_ref[:, columns(2 * n_head + target, size)] * total).astype(BF16)


def concat_kernel(a_ref, b_ref, out_ref):
    half = a_ref.shape[0]
    out_ref[:half] = a_ref[...]
    out_ref[half:] = b_ref[...]


def place_kernel(half, meta_ref, *refs):
    pieces, out, sems = refs[-2 - len(ROWS) : -2], refs[-2], refs[-1]
    size = pieces[0].shape[2]
    copies = []
    for c, (piece, part) in enumerate(zip(pieces, ROWS)):
        for spot, step in enumerate(combos(ORDERS[c])[4 * half : 4 * half + 4]):
            to = out.at[pl.ds(rows_of(c).start, part), columns(meta_ref[1] ^ step, size)]
            copies.append(pltpu.make_async_copy(piece.at[spot], to, sems.at[len(copies)]))
            copies[-1].start()
    for copy in copies:
        copy.wait()


def body(latents, levels, counts, window_mask, modulation, qkv_weight, out_weight):
    rows, width = latents.shape
    size = qkv_weight.shape[2]
    weight = jnp.transpose(qkv_weight, (1, 0, 2))
    n_head = lax.axis_size("head")
    n_queue = lax.axis_size("queue")
    meta = jnp.stack([lax.axis_index("queue"), lax.axis_index("head")]).astype(jnp.int32)
    shape = jax.ShapeDtypeStruct

    def swap(array, chain, level):
        step = ORDERS[chain][level]
        return lax.ppermute(array, "head", [(i, i ^ step) for i in range(n_head)])

    kv, table = pl.pallas_call(
        keys_kernel,
        out_shape=(shape((2, rows, size), BF16), shape((1, 3 * width), F32)),
        in_specs=smem() + hbm(3),
        out_specs=vmem(2),
        scratch_shapes=[
            pltpu.VMEM((rows, width), BF16),
            pltpu.VMEM((rows, width), BF16),
            pltpu.VMEM((8, 3 * width), F32),
            pltpu.VMEM((2, width, size), BF16),
            pltpu.SemaphoreType.DMA((3 + LOADS,)),
        ],
        compiler_params=params(53),
        cost_estimate=cost(4 * rows * width * size, 4 * width * size),
    )(levels, latents, modulation, weight)

    chip = lax.ppermute(kv, "queue", [(i, i ^ 1) for i in range(n_queue)])
    route = []
    for i in range(n_queue):
        j = i - 1 + i % 2 * 2
        for k in range(n_head):
            there = j * n_head + k if 0 <= j < n_queue else i * n_head + (k ^ 1)
            route.append((i * n_head + k, there))
    cross = lax.ppermute(kv, ("queue", "head"), route)

    query, *state = pl.pallas_call(
        near_kernel,
        out_shape=(shape((rows, size), BF16),) + (shape((rows, size), F32),) * 3,
        in_specs=smem(3) + hbm() + vmem() + hbm() + vmem(2),
        out_specs=vmem(4),
        scratch_shapes=[
            pltpu.VMEM((rows, width), BF16),
            pltpu.VMEM((rows, width), BF16),
            pltpu.VMEM((width, size), BF16),
            pltpu.SemaphoreType.DMA((1 + LOADS,)),
        ],
        compiler_params=params(NEAR),
        cost_estimate=cost(1, 1),
    )(meta, counts, window_mask.T, latents, table, weight, kv, chip)

    held = [2 if half else 4 for half in HALVES]
    parts = pl.pallas_call(
        join_kernel,
        out_shape=tuple(shape((n, part, size), BF16) for n, part in zip(held, ROWS) for _ in range(8 // n)),
        in_specs=smem(3) + vmem(6),
        out_specs=(vmem()[0],) * sum(8 // n for n in held),
        scratch_shapes=[pltpu.VMEM((rows, size), BF16)],
        compiler_params=params(32),
        cost_estimate=cost(4 * rows * width * size, 2 * width * size),
    )(meta, counts, window_mask.T, query, *state, cross, out_weight)

    small = dict(compiler_params=params(16), cost_estimate=cost(4 * 96 * size, 8 * 96 * size))

    def add(part, *terms):
        return pl.pallas_call(
            functools.partial(add_kernel, [start for start, _ in terms]),
            out_shape=shape((2, part, size), BF16),
            in_specs=vmem(len(terms)),
            out_specs=vmem()[0],
            **small,
        )(*[term for _, term in terms])

    chains = range(len(ROWS))
    keep, pass_on, got, got_on = {}, {}, {}, {}
    for c in chains:
        if HALVES[c]:
            keep[c], pass_on[c], give, give_on = parts[:4]
            parts = parts[4:]
            got_on[c] = swap(give_on, c, 0)
            got[c] = swap(give, c, 0)
        else:
            keep[c], give = parts[:2]
            parts = parts[2:]
            got[c] = swap(give, c, 0)
    relayed = {}
    for c, part in enumerate(ROWS):
        if HALVES[c]:
            term = add(part, (0, pass_on[c]), (0, got_on[c]))
        else:
            term = add(part, (2, keep[c]), (2, got[c]))
        relayed[c] = swap(term, c, 1)
    mine, other = {}, {}
    for c, part in enumerate(ROWS):
        mine[c] = add(part, (0, keep[c]), (0, got[c]), (0, relayed[c]))
        other[c] = swap(mine[c], c, 2)
    moved = {}
    for c, part in enumerate(ROWS):
        fresh = pl.pallas_call(
            functools.partial(update_kernel, c),
            out_shape=shape((2, part, size), BF16),
            in_specs=smem() + vmem(4),
            out_specs=vmem()[0],
            **small,
        )(meta, latents, table, mine[c], other[c])
        moved[c] = lax.ppermute(fresh, "queue", [(i, (i - 1) % n_queue) for i in range(n_queue)])
    ready = []
    for c, part in enumerate(ROWS):
        near = swap(moved[c], c, 1)
        if GATHER[c]:
            ready += [moved[c], near, swap(moved[c], c, 0), swap(near, c, 0)]
        else:
            four = pl.pallas_call(
                concat_kernel,
                out_shape=shape((4, part, size), BF16),
                in_specs=vmem(2),
                out_specs=vmem()[0],
                **small,
            )(moved[c], near)
            ready += [four, swap(four, c, 0)]

    out = []
    for half in range(2):
        out = [
            pl.pallas_call(
                functools.partial(place_kernel, half),
                out_shape=shape((rows, width), BF16),
                in_specs=smem() + hbm(len(out)) + vmem(len(ROWS)),
                out_specs=hbm()[0],
                scratch_shapes=[pltpu.SemaphoreType.DMA((4 * len(ROWS),))],
                input_output_aliases={1: 0} if out else {},
                **small,
            )(meta, *out, *ready[half::2])
        ]
    return out[0]


def solution(mesh):
    in_specs = (P("queue", None), P("queue"), P(), P(), P(), P(None, None, "head"), P("head", None))
    out_specs = P("queue", None)
    return jax.shard_map(body, mesh=mesh, in_specs=in_specs, out_specs=out_specs, check_vma=False)
```

```python
import functools
import math

import jax
import jax.numpy as jnp
from jax import lax
from jax.experimental import pallas as pl
from jax.experimental.pallas import tpu as pltpu
from jax.sharding import PartitionSpec as P

HD = 128
ROWS = (96, 96, 96)
ORDERS = ((1, 4, 3), (3, 1, 4), (4, 3, 1))
HALVES = (True, True, True)
GATHER = (True, False, False)
CHUNK = 16
LOADS = 3
NEAR = 48
F32, BF16 = jnp.float32, jnp.bfloat16


def vmem(n=1):
    return [pl.BlockSpec(memory_space=pltpu.VMEM)] * n


def smem(n=1):
    return [pl.BlockSpec(memory_space=pltpu.SMEM)] * n


def hbm(n=1):
    return [pl.BlockSpec(memory_space=pltpu.HBM)] * n


def params(mib):
    return pltpu.CompilerParams(vmem_limit_bytes=mib * 1024 * 1024)


def cost(flops, size):
    return pl.CostEstimate(flops=flops, bytes_accessed=size, transcendentals=0)


def dot(a, b):
    return jnp.dot(a, b, preferred_element_type=F32)


def dot_t(a, b):
    return lax.dot_general(a, b, (((1,), (1,)), ((), ())), preferred_element_type=F32)


def combos(dims):
    found = [0]
    for d in dims:
        found = [f ^ e for f in found for e in (0, d)]
    return found


def rows_of(chain):
    start = sum(ROWS[:chain])
    return slice(start, start + ROWS[chain])


def columns(target, size):
    return pl.ds(pl.multiple_of(target * size, size), size)


def load(pieces, target, sems, first):
    part = target.shape[0] // LOADS
    copies = []
    for i in range(LOADS):
        at = pl.ds(i * part, part)
        copies.append(pltpu.make_async_copy(pieces.at[at], target.at[at], sems.at[first + i]))
        copies[-1].start()
    return copies


def normalize(copies, x_ref, mod_ref, row, normed_ref):
    rows, width = x_ref.shape

    def step(i, carry):
        at = pl.ds(pl.multiple_of(i * CHUNK, CHUNK), CHUNK)
        x = x_ref[at, :].astype(F32)
        mean = jnp.mean(x, axis=-1, keepdims=True)
        centered = x - mean
        variance = jnp.mean(centered * centered, axis=-1, keepdims=True)
        scaled = centered * lax.rsqrt(variance + 1e-06)
        normed = scaled * (1.0 + mod_ref[row, width : 2 * width]) + mod_ref[row, :width]
        normed_ref[at, :] = normed.astype(BF16)
        return carry

    steps = rows // LOADS // CHUNK
    for i, copy in enumerate(copies):
        copy.wait()
        lax.fori_loop(i * steps, (i + 1) * steps, step, 0, unroll=steps)


def keys_kernel(level_ref, x_hbm, mod_hbm, w_hbm, kv_ref, table_ref, x_ref, normed_ref, mod_ref, w_ref, sems):
    level = level_ref[0]
    first = pl.multiple_of(level // 8 * 8, 8)
    copy_mod = pltpu.make_async_copy(mod_hbm.at[pl.ds(first, 8)], mod_ref, sems.at[0])
    copy_k = pltpu.make_async_copy(w_hbm.at[1], w_ref.at[0], sems.at[1])
    copy_v = pltpu.make_async_copy(w_hbm.at[2], w_ref.at[1], sems.at[2])
    copy_mod.start()
    copies = load(x_hbm, x_ref, sems, 3)
    copy_k.start()
    copy_v.start()
    copy_mod.wait()
    row = pl.ds(level % 8, 1)
    normalize(copies, x_ref, mod_ref, row, normed_ref)
    table_ref[...] = mod_ref[row, :]
    copy_k.wait()
    kv_ref[0] = dot(normed_ref[...], w_ref[0]).astype(BF16)
    copy_v.wait()
    kv_ref[1] = dot(normed_ref[...], w_ref[1]).astype(BF16)


def masked(scores, limit):
    spots = lax.broadcasted_iota(jnp.int32, scores.shape, 1)
    return jnp.where(spots < limit, scores * (1.0 / math.sqrt(HD)), -jnp.inf)


def limits(place, counts_ref, mask_ref):
    places = counts_ref.shape[0]
    before = jnp.where(place > 0, counts_ref[jnp.maximum(place - 1, 0)] * mask_ref[0, place], 0)
    after = jnp.where(
        place < places - 1, counts_ref[jnp.minimum(place + 1, places - 1)] * mask_ref[1, place], 0
    )
    odd = place % 2 == 1
    return jnp.where(odd, before, after), jnp.where(odd, after, before)


def near_kernel(
    meta_ref, counts_ref, mask_ref, x_hbm, table_ref, w_hbm, kv_ref, chip_ref, q_ref, o_ref, m_ref, l_ref, *scratch
):
    x_ref, normed_ref, w_ref, sems = scratch
    rows, size = q_ref.shape
    copies = load(x_hbm, x_ref, sems, 1)
    copy_q = pltpu.make_async_copy(w_hbm.at[0], w_ref, sems.at[0])
    copy_q.start()
    normalize(copies, x_ref, table_ref, slice(0, 1), normed_ref)
    copy_q.wait()
    q_ref[...] = dot(normed_ref[...], w_ref[...]).astype(BF16)
    place = meta_ref[0]
    own = counts_ref[place]
    chip = limits(place, counts_ref, mask_ref)[0]
    for head in range(size // HD):
        at = slice(head * HD, (head + 1) * HD)
        query = q_ref[:, at]
        left = masked(dot_t(query, kv_ref[0, :, at]), own)
        right = masked(dot_t(query, chip_ref[0, :, at]), chip)
        top = jnp.max(jnp.maximum(left, right), axis=-1, keepdims=True)
        left = jnp.exp(left - top)
        right = jnp.exp(right - top)
        m_ref[:, at] = jnp.broadcast_to(top, (rows, HD))
        l_ref[:, at] = jnp.broadcast_to(jnp.sum(left + right, axis=-1, keepdims=True), (rows, HD))
        o_ref[:, at] = dot(left.astype(BF16), kv_ref[1, :, at]) + dot(right.astype(BF16), chip_ref[1, :, at])


def join_kernel(meta_ref, counts_ref, mask_ref, q_ref, o_ref, m_ref, l_ref, far_ref, w_ref, *refs):
    outs, att_ref = refs[:-1], refs[-1]
    h = meta_ref[1]
    limit = limits(meta_ref[0], counts_ref, mask_ref)[1]
    rows, size = q_ref.shape
    for head in range(size // HD):
        at = slice(head * HD, (head + 1) * HD)
        scores = masked(dot_t(q_ref[:, at], far_ref[0, :, at]), limit)
        old = m_ref[:, at][:, :1]
        top = jnp.maximum(old, jnp.max(scores, axis=-1, keepdims=True))
        expo = jnp.exp(scores - top)
        keep = jnp.exp(old - top)
        total = l_ref[:, at][:, :1] * keep + jnp.sum(expo, axis=-1, keepdims=True)
        acc = o_ref[:, at] * keep + dot(expo.astype(BF16), far_ref[1, :, at])
        att_ref[:, at] = (acc / total).astype(BF16)
    for k in range(w_ref.shape[1] // size):
        result = dot(att_ref[...], w_ref[:, columns(h ^ k, size)]).astype(BF16)
        first = 0
        for c, dims in enumerate(ORDERS):
            spot = combos(dims).index(k)
            held = outs[first].shape[0]
            outs[first + spot // held][spot % held] = result[rows_of(c)]
            first += 8 // held


def add_kernel(starts, *refs):
    total = 0.0
    for start, ref in zip(starts, refs):
        total = total + ref[start : start + 2].astype(F32)
    refs[-1][...] = total.astype(BF16)


def update_kernel(chain, meta_ref, x_ref, table_ref, keep_ref, got_ref, out_ref):
    size = out_ref.shape[2]
    n_head = x_ref.shape[1] // size
    for j in range(2):
        target = meta_ref[1] ^ combos(ORDERS[chain])[j]
        at = columns(target, size)
        total = keep_ref[j].astype(F32) + got_ref[1 - j].astype(F32)
        x = x_ref[rows_of(chain), at].astype(F32)
        out_ref[j] = (x + table_ref[:, columns(2 * n_head + target, size)] * total).astype(BF16)


def concat_kernel(a_ref, b_ref, out_ref):
    half = a_ref.shape[0]
    out_ref[:half] = a_ref[...]
    out_ref[half:] = b_ref[...]


def place_kernel(plan, meta_ref, *refs):
    pieces, out, sems = refs[-2 - len(plan) : -2], refs[-2], refs[-1]
    size = pieces[0].shape[2]
    copies = []
    for (c, first), piece in zip(plan, pieces):
        for i in range(piece.shape[0]):
            target = meta_ref[1] ^ combos(ORDERS[c])[first + i]
            to = out.at[pl.ds(rows_of(c).start, ROWS[c]), columns(target, size)]
            copies.append(pltpu.make_async_copy(piece.at[i], to, sems.at[len(copies)]))
            copies[-1].start()
    for copy in copies:
        copy.wait()


def body(latents, levels, counts, window_mask, modulation, qkv_weight, out_weight):
    rows, width = latents.shape
    size = qkv_weight.shape[2]
    weight = jnp.transpose(qkv_weight, (1, 0, 2))
    n_head = lax.axis_size("head")
    n_queue = lax.axis_size("queue")
    meta = jnp.stack([lax.axis_index("queue"), lax.axis_index("head")]).astype(jnp.int32)
    shape = jax.ShapeDtypeStruct

    def swap(array, chain, level):
        step = ORDERS[chain][level]
        return lax.ppermute(array, "head", [(i, i ^ step) for i in range(n_head)])

    kv, table = pl.pallas_call(
        keys_kernel,
        out_shape=(shape((2, rows, size), BF16), shape((1, 3 * width), F32)),
        in_specs=smem() + hbm(3),
        out_specs=vmem(2),
        scratch_shapes=[
            pltpu.VMEM((rows, width), BF16),
            pltpu.VMEM((rows, width), BF16),
            pltpu.VMEM((8, 3 * width), F32),
            pltpu.VMEM((2, width, size), BF16),
            pltpu.SemaphoreType.DMA((3 + LOADS,)),
        ],
        compiler_params=params(53),
        cost_estimate=cost(4 * rows * width * size, 4 * width * size),
    )(levels, latents, modulation, weight)

    chip = lax.ppermute(kv, "queue", [(i, i ^ 1) for i in range(n_queue)])
    route = []
    for i in range(n_queue):
        j = i - 1 + i % 2 * 2
        for k in range(n_head):
            there = j * n_head + k if 0 <= j < n_queue else i * n_head + (k ^ 1)
            route.append((i * n_head + k, there))
    cross = lax.ppermute(kv, ("queue", "head"), route)

    query, *state = pl.pallas_call(
        near_kernel,
        out_shape=(shape((rows, size), BF16),) + (shape((rows, size), F32),) * 3,
        in_specs=smem(3) + hbm() + vmem() + hbm() + vmem(2),
        out_specs=vmem(4),
        scratch_shapes=[
            pltpu.VMEM((rows, width), BF16),
            pltpu.VMEM((rows, width), BF16),
            pltpu.VMEM((width, size), BF16),
            pltpu.SemaphoreType.DMA((1 + LOADS,)),
        ],
        compiler_params=params(NEAR),
        cost_estimate=cost(1, 1),
    )(meta, counts, window_mask.T, latents, table, weight, kv, chip)

    held = [2 if half else 4 for half in HALVES]
    parts = pl.pallas_call(
        join_kernel,
        out_shape=tuple(shape((n, part, size), BF16) for n, part in zip(held, ROWS) for _ in range(8 // n)),
        in_specs=smem(3) + vmem(6),
        out_specs=(vmem()[0],) * sum(8 // n for n in held),
        scratch_shapes=[pltpu.VMEM((rows, size), BF16)],
        compiler_params=params(32),
        cost_estimate=cost(4 * rows * width * size, 2 * width * size),
    )(meta, counts, window_mask.T, query, *state, cross, out_weight)

    small = dict(compiler_params=params(16), cost_estimate=cost(4 * 96 * size, 8 * 96 * size))

    def add(part, *terms):
        return pl.pallas_call(
            functools.partial(add_kernel, [start for start, _ in terms]),
            out_shape=shape((2, part, size), BF16),
            in_specs=vmem(len(terms)),
            out_specs=vmem()[0],
            **small,
        )(*[term for _, term in terms])

    chains = range(len(ROWS))
    keep, pass_on, got, got_on = {}, {}, {}, {}
    for c in chains:
        if HALVES[c]:
            keep[c], pass_on[c], give, give_on = parts[:4]
            parts = parts[4:]
            got_on[c] = swap(give_on, c, 0)
            got[c] = swap(give, c, 0)
        else:
            keep[c], give = parts[:2]
            parts = parts[2:]
            got[c] = swap(give, c, 0)
    relayed = {}
    for c, part in enumerate(ROWS):
        if HALVES[c]:
            term = add(part, (0, pass_on[c]), (0, got_on[c]))
        else:
            term = add(part, (2, keep[c]), (2, got[c]))
        relayed[c] = swap(term, c, 1)
    mine, other = {}, {}
    for c, part in enumerate(ROWS):
        mine[c] = add(part, (0, keep[c]), (0, got[c]), (0, relayed[c]))
        other[c] = swap(mine[c], c, 2)
    moved = {}
    for c, part in enumerate(ROWS):
        fresh = pl.pallas_call(
            functools.partial(update_kernel, c),
            out_shape=shape((2, part, size), BF16),
            in_specs=smem() + vmem(4),
            out_specs=vmem()[0],
            **small,
        )(meta, latents, table, mine[c], other[c])
        moved[c] = lax.ppermute(fresh, "queue", [(i, (i - 1) % n_queue) for i in range(n_queue)])
    ready = [[], []]
    for c, part in enumerate(ROWS):
        near = swap(moved[c], c, 1)
        if GATHER[c]:
            ready[0] += [((c, 0), moved[c]), ((c, 2), near)]
            ready[1] += [((c, 4), swap(moved[c], c, 0)), ((c, 6), swap(near, c, 0))]
        else:
            four = pl.pallas_call(
                concat_kernel,
                out_shape=shape((4, part, size), BF16),
                in_specs=vmem(2),
                out_specs=vmem()[0],
                **small,
            )(moved[c], near)
            ready[0] += [((c, 0), four)]
            ready[1] += [((c, 4), swap(four, c, 0))]

    out = []
    for group in ready:
        plan, pieces = zip(*group)
        out = [
            pl.pallas_call(
                functools.partial(place_kernel, plan),
                out_shape=shape((rows, width), BF16),
                in_specs=smem() + hbm(len(out)) + vmem(len(pieces)),
                out_specs=hbm()[0],
                scratch_shapes=[pltpu.SemaphoreType.DMA((4 * len(ROWS),))],
                input_output_aliases={1: 0} if out else {},
                **small,
            )(meta, *out, *pieces)
        ]
    return out[0]


def solution(mesh):
    in_specs = (P("queue", None), P("queue"), P(), P(), P(), P(None, None, "head"), P("head", None))
    out_specs = P("queue", None)
    return jax.shard_map(body, mesh=mesh, in_specs=in_specs, out_specs=out_specs, check_vma=False)
```
